256 devices in a mesh: row: 128 (over z, y_lo, x, core), col: 2 (over y_hi).
Axes of the slice: x: 4, y: 4 (y_hi: 2, y_lo: 2; y = y_hi * 2 + y_lo), z: 8, core: 2. Of those that a mesh axis runs over, the one named last changes fastest.
Arguments:
- matrix_panel: bfloat16 [128, 1048576], P('col', 'row'), may hold values from -6 to 6
- row_signs: int32 [1048576], P('row'), may hold values from -1 to 1, as said below
- sample_rows: int32 [16384], replicated, may hold values from 0 to 1048575, as said below
Outputs:
- sketch: float32 [128, 16384], P('col', 'row')
- gram: float32 [128, 128], P('col')
The draws below stay inside these ranges and needn't reach their ends.
Inputs may be any that keep to these rules, and one draw needn't show every extreme that they name: `row_signs`: each entry is -1 or +1. `sample_rows`: strictly increasing, so all distinct.
All inputs are finite; a program needn't handle non-finite values.
Results may differ from the reference program's by a relative error of at most 0.0003.
Values sent between devices are 32-bit elements; how exact they have to be, the bound alone decides.
A program may use at most 64 MiB of HBM per device.

```python
import jax
import jax.numpy as jnp
from jax import lax

PANEL = 128
ROWS_DEV = 8192
LENGTH = 1048576
SAMPLES = 16384
N_ROW = 128


def draw_row_signs(key, part):
    return (jax.random.randint(key, (LENGTH,), 0, 2) * 2 - 1).astype(jnp.int32)


def draw_sample_rows(key, part):
    picked = jax.random.choice(jax.random.fold_in(key, 7), LENGTH, (SAMPLES,), replace=False)
    return jnp.sort(picked.astype(jnp.int32))


def levels(own_key, extent, shards, smallest, top_value):
    def one(dim, blocks):
        heights = jax.random.uniform(jax.random.fold_in(jax.random.fold_in(own_key, 6), dim), (blocks,), jnp.float32, smallest / len(shards), top_value / len(shards))
        return jnp.repeat(jnp.exp(heights), extent[dim] // blocks).reshape((-1,) + (1,) * (len(extent) - dim - 1))

    loudness = one(*shards[0])
    for cut in shards[1:]:
        loudness = loudness * one(*cut)
    return loudness


def noise(key, shape, spread, bound, shards=(), kind=jnp.bfloat16):
    factor_of = levels(key, shape, shards, -0.22, 0.18) if shards else 1.0
    result = jax.random.normal(key, shape, jnp.float32) * spread * factor_of
    return jnp.minimum(jnp.maximum(result, -bound), bound).astype(kind)


def setup_inputs(seed: int = 0) -> dict:
    splits = jax.random.split(jax.random.key(seed), 4)
    return {
        "matrix_panel": noise(splits[0], (PANEL, LENGTH), 1.0, 6.0, ((0, 2), (1, 128))),
        "row_signs": draw_row_signs(jax.random.fold_in(splits[3], 71), 0),
        "sample_rows": draw_sample_rows(jax.random.fold_in(splits[3], 71), 0),
    }


def parity_sign(left, right, bit_count):
    common = jnp.bitwise_and(left, right)
    total = jnp.zeros_like(common)
    for bit_index in range(bit_count):
        total = total + jnp.bitwise_and(jnp.right_shift(common, bit_index), 1)
    return (1 - 2 * jnp.bitwise_and(total, 1)).astype(jnp.float32)

def hadamard(order_size):
    bit_count = order_size.bit_length() - 1
    row_index = jnp.arange(order_size, dtype=jnp.int32)
    return parity_sign(row_index[:, None], row_index[None, :], bit_count)

def local_mix(block, signs):
    columns, length = block.shape
    first_size = min(length, 256)
    second_size = length // first_size
    values = block.astype(jnp.float32) * signs.astype(jnp.float32)[None, :]
    values = values.reshape(columns, first_size, second_size)
    values = jnp.einsum('cab,ad->cdb', values, hadamard(first_size), precision=lax.Precision.HIGHEST)
    values = jnp.einsum('cdb,be->cde', values, hadamard(second_size), precision=lax.Precision.HIGHEST)
    return values.reshape(columns, length) / jnp.sqrt(jnp.float32(length))

def reference(matrix_panel, row_signs, sample_rows):
    bit_count = N_ROW.bit_length() - 1
    owner = sample_rows // ROWS_DEV
    offset = sample_rows - owner * ROWS_DEV

    def accumulate(carry, block_index):
        start = (block_index * ROWS_DEV).astype(jnp.int32)
        block = lax.dynamic_slice_in_dim(matrix_panel, start, ROWS_DEV, 1)
        signs = lax.dynamic_slice_in_dim(row_signs, start, ROWS_DEV, 0)
        mixed = local_mix(block, signs)
        chosen = jnp.take(mixed, offset, axis=1)
        weights = parity_sign(owner, block_index, bit_count)
        return (carry + chosen * weights[None, :], None)
    initial = jnp.zeros((PANEL, SAMPLES), jnp.float32)
    summed, _ = lax.scan(accumulate, initial, jnp.arange(N_ROW, dtype=jnp.int32))
    sketch = summed / jnp.sqrt(jnp.float32(N_ROW))
    gram = jnp.dot(sketch, sketch.T, precision=lax.Precision.HIGHEST) / SAMPLES
    return (sketch, gram)
```

```python
import functools

import jax
import jax.numpy as jnp
from jax import lax
from jax.experimental import pallas as pl
from jax.experimental.pallas import tpu as pltpu
from jax.sharding import PartitionSpec as P

MESH = pl.DeviceIdType.MESH
Z = 8
PLANE = 8
CORES = 2
BLOCK = 128
COLS = 64
SPLIT = 4
DEPTH = 2048
CHUNK = PLANE * CORES * BLOCK


def parity(value, shift):
    while shift:
        value = value ^ (value >> shift)
        shift //= 2
    return value & 1


def sign_of(odd):
    return (1 - 2 * odd).astype(jnp.float32)


def mixed_chunk(position, rows, x_ref):
    count = rows.shape[1]
    bit = lambda k: sign_of((rows >> k) & 1)
    wide = lambda k: jnp.broadcast_to(bit(k), (16, count)).astype(jnp.bfloat16)
    spread = jnp.broadcast_to(rows, (16, count))
    low = parity(spread & lax.broadcasted_iota(jnp.int32, (16, count), 0), 2)
    tiles = [sign_of(low).astype(jnp.bfloat16)]
    for k in range(4, 8):
        flip = wide(k)
        tiles = tiles + [tile * flip for tile in tiles]
    upper = [None]
    for k in range(8, 11):
        flip = wide(k)
        upper = upper + [flip if one is None else one * flip for one in upper]
    total = jnp.zeros((SPLIT * COLS, count), jnp.float32)
    for k, flip in enumerate(upper):
        signs = jnp.concatenate([tile if flip is None else tile * flip for tile in tiles], axis=0)
        total = total + jnp.dot(
            x_ref[:, k * 256:(k + 1) * 256], signs, preferred_element_type=jnp.float32
        )
    parts = [total[a * COLS:(a + 1) * COLS] for a in range(SPLIT)]
    for k in (11, 12):
        flip = bit(k)
        parts = [parts[2 * i] + flip * parts[2 * i + 1] for i in range(len(parts) // 2)]
    weight = sign_of(parity((rows >> 13) & position, 4)) * (1.0 / 1024.0)
    return parts[0] * weight


def kernel(
    x_ref, sign_ref, rows_ref, sketch_ref, gram_ref,
    xs, part, got_core, summed, got_plane, send_z, got_z, both, gram_part, got_rs, totals, pieces,
    core_send, core_recv, plane_send, plane_recv, z_send, z_recv,
    col_sem, rs_send, rs_recv, tot_send, tot_recv, out_send, out_recv,
):
    position = lax.axis_index("row")
    col = lax.axis_index("col")
    z = position // 16
    mine = (position // 2) % 8
    core = position % 2

    def device(z_at, plane_at, core_at):
        return (z_at * 16 + plane_at * 2 + core_at, col)

    def z_core(k):
        other = (z * 2 + core + k) % 16
        return other, device(other // 2, mine, other % 2)

    barrier = pltpu.get_barrier_semaphore()
    for d in range(1, PLANE):
        pl.semaphore_signal(barrier, inc=1, device_id=device(z, mine ^ d, core), device_id_type=MESH)
    for k in range(1, 16):
        pl.semaphore_signal(barrier, inc=1, device_id=z_core(k)[1], device_id_type=MESH)
    pl.semaphore_signal(barrier, inc=1, device_id=(position, 1 - col), device_id_type=MESH)

    for a in range(SPLIT):
        window = slice(a * DEPTH, (a + 1) * DEPTH)
        xs[a * COLS:(a + 1) * COLS, :] = (
            x_ref[:, window].astype(jnp.float32) * sign_ref[:, window].astype(jnp.float32)
        ).astype(jnp.bfloat16)

    pl.semaphore_wait(barrier, 23)

    def target(t):
        return (z + jnp.where(t % 2 == 0, 4 + t // 2, 4 - (t + 1) // 2)) % Z

    def core_copy(t):
        return pltpu.make_async_remote_copy(
            src_ref=part.at[t, 1 - core], dst_ref=got_core.at[t],
            send_sem=core_send.at[t], recv_sem=core_recv.at[t],
            device_id=device(z, mine, 1 - core), device_id_type=MESH,
        )

    def plane_copy(t, d):
        return pltpu.make_async_remote_copy(
            src_ref=summed.at[t, mine ^ d], dst_ref=got_plane.at[t, d - 1],
            send_sem=plane_send.at[t, d - 1], recv_sem=plane_recv.at[t, d - 1],
            device_id=device(z, mine ^ d, core), device_id_type=MESH,
        )

    def z_copy(t):
        return pltpu.make_async_remote_copy(
            src_ref=send_z.at[t], dst_ref=got_z.at[t],
            send_sem=z_send.at[t], recv_sem=z_recv.at[t],
            device_id=device(target(t), mine, core), device_id_type=MESH,
        )

    def compute(t):
        start = pl.multiple_of(target(t) * CHUNK, CHUNK)
        chunk = mixed_chunk(position, rows_ref[:, pl.ds(start, CHUNK)], xs)
        for j in range(16):
            part[t, j % 2, j // 2] = chunk[:, j * BLOCK:(j + 1) * BLOCK]
        core_copy(t).start()

    def plane_stage(t):
        core_copy(t).wait_recv()
        summed[t] = part[t, core] + got_core[t]
        for d in range(1, PLANE):
            plane_copy(t, d).start()

    def z_stage(t):
        for d in range(1, PLANE):
            plane_copy(t, d).wait_recv()
        block = summed[t, mine]
        for d in range(1, PLANE):
            block = block + got_plane[t, d - 1]
        send_z[t] = block

    def step(t, carry):
        @pl.when(t < Z)
        def _():
            compute(t)

        @pl.when((t >= 1) & (t <= Z))
        def _():
            plane_stage(t - 1)

        @pl.when(t >= 2)
        def _():
            z_stage(t - 2)

        @pl.when((t >= 2) & (t <= Z))
        def _():
            z_copy(t - 2).start()

        return carry

    lax.fori_loop(0, Z + 2, step, 0)

    own = send_z[Z - 1]
    for t in range(Z - 1):
        z_copy(t).wait_recv()
        own = own + got_z[t]
    sketch_ref[...] = own

    place = pl.ds(pl.multiple_of(col * COLS, COLS), COLS)
    both[place, :] = own
    col_copy = pltpu.make_async_remote_copy(
        src_ref=both.at[place], dst_ref=both.at[place],
        send_sem=col_sem.at[0], recv_sem=col_sem.at[1],
        device_id=(position, 1 - col), device_id_type=MESH,
    )
    col_copy.start()
    other = pl.ds(pl.multiple_of((1 - col) * COLS, COLS), COLS)
    pltpu.make_async_remote_copy(
        src_ref=both.at[other], dst_ref=both.at[other],
        send_sem=col_sem.at[0], recv_sem=col_sem.at[1],
        device_id=(position, 1 - col), device_id_type=MESH,
    ).wait_recv()
    gram_part[...] = lax.dot_general(
        own, both[...], (((1,), (1,)), ((), ())),
        precision=lax.Precision.HIGHEST, preferred_element_type=jnp.float32,
    ).reshape(PLANE, 8, 128)

    def rs_copy(d):
        return pltpu.make_async_remote_copy(
            src_ref=gram_part.at[mine ^ d], dst_ref=got_rs.at[d - 1],
            send_sem=rs_send.at[d - 1], recv_sem=rs_recv.at[d - 1],
            device_id=device(z, mine ^ d, core), device_id_type=MESH,
        )

    for d in range(1, PLANE):
        rs_copy(d).start()
    for d in range(1, PLANE):
        rs_copy(d).wait_recv()
    piece = gram_part[mine]
    for d in range(1, PLANE):
        piece = piece + got_rs[d - 1]
    me = z * 2 + core
    totals[me] = piece

    def tot_copy(k, to):
        return pltpu.make_async_remote_copy(
            src_ref=totals.at[me], dst_ref=totals.at[me],
            send_sem=tot_send.at[k - 1], recv_sem=tot_recv.at[k - 1],
            device_id=to, device_id_type=MESH,
        )

    for k in range(1, 16):
        tot_copy(k, z_core(k)[1]).start()
    for k in range(1, 16):
        sender = (me + 16 - k) % 16
        pltpu.make_async_remote_copy(
            src_ref=totals.at[sender], dst_ref=totals.at[sender],
            send_sem=tot_send.at[k - 1], recv_sem=tot_recv.at[k - 1],
            device_id=z_core(k)[1], device_id_type=MESH,
        ).wait_recv()
    piece = totals[0]
    for k in range(1, 16):
        piece = piece + totals[k]
    pieces[mine] = piece * (1.0 / 16384.0)

    def out_copy(d, at):
        return pltpu.make_async_remote_copy(
            src_ref=pieces.at[at], dst_ref=pieces.at[at],
            send_sem=out_send.at[d - 1], recv_sem=out_recv.at[d - 1],
            device_id=device(z, mine ^ d, core), device_id_type=MESH,
        )

    for d in range(1, PLANE):
        out_copy(d, mine).start()
    for d in range(1, PLANE):
        out_copy(d, mine ^ d).wait_recv()
    gram_ref[...] = pieces[...].reshape(COLS, 128)

    def drain(t, carry):
        core_copy(t).wait_send()
        for d in range(1, PLANE):
            plane_copy(t, d).wait_send()

        @pl.when(t < Z - 1)
        def _():
            z_copy(t).wait_send()

        return carry

    lax.fori_loop(0, Z, drain, 0)
    col_copy.wait_send()
    for d in range(1, PLANE):
        rs_copy(d).wait_send()
        out_copy(d, mine).wait_send()
    for k in range(1, 16):
        tot_copy(k, z_core(k)[1]).wait_send()


def body(matrix_panel, row_signs, sample_rows):
    vmem = pl.BlockSpec(memory_space=pltpu.VMEM)
    f32 = jnp.float32
    block = (COLS, BLOCK)
    sems = pltpu.SemaphoreType.DMA
    return pl.pallas_call(
        kernel,
        out_shape=(jax.ShapeDtypeStruct(block, f32), jax.ShapeDtypeStruct(block, f32)),
        in_specs=[vmem] * 3,
        out_specs=(vmem, vmem),
        scratch_shapes=[
            pltpu.VMEM((SPLIT * COLS, DEPTH), jnp.bfloat16),
            pltpu.VMEM((Z, CORES, PLANE) + block, f32),
            pltpu.VMEM((Z, PLANE) + block, f32),
            pltpu.VMEM((Z, PLANE) + block, f32),
            pltpu.VMEM((Z, PLANE - 1) + block, f32),
            pltpu.VMEM((Z,) + block, f32),
            pltpu.VMEM((Z - 1,) + block, f32),
            pltpu.VMEM((2 * COLS, BLOCK), f32),
            pltpu.VMEM((PLANE, 8, 128), f32),
            pltpu.VMEM((PLANE - 1, 8, 128), f32),
            pltpu.VMEM((16, 8, 128), f32),
            pltpu.VMEM((PLANE, 8, 128), f32),
            sems((Z,)), sems((Z,)),
            sems((Z, PLANE - 1)), sems((Z, PLANE - 1)),
            sems((Z - 1,)), sems((Z - 1,)),
            sems((2,)),
            sems((PLANE - 1,)), sems((PLANE - 1,)),
            sems((15,)), sems((15,)),
            sems((PLANE - 1,)), sems((PLANE - 1,)),
        ],
        compiler_params=pltpu.CompilerParams(
            collective_id=0, has_side_effects=True, vmem_limit_bytes=56 * 2**20
        ),
        cost_estimate=pl.CostEstimate(
            flops=2 * COLS * 8192 * 16384, bytes_accessed=2**21, transcendentals=0
        ),
    )(matrix_panel, row_signs.reshape(1, -1), sample_rows.reshape(1, -1))


def solution(mesh):
    return jax.shard_map(
        body,
        mesh=mesh,
        in_specs=(P("col", "row"), P("row"), P()),
        out_specs=(P("col", "row"), P("col", None)),
        check_vma=False,
    )
```

```python
import functools

import jax
import jax.numpy as jnp
from jax import lax
from jax.experimental import pallas as pl
from jax.experimental.pallas import tpu as pltpu
from jax.sharding import PartitionSpec as P

MESH = pl.DeviceIdType.MESH
Z = 8
PLANE = 8
CORES = 2
BLOCK = 128
COLS = 64
SPLIT = 4
DEPTH = 2048
CHUNK = PLANE * CORES * BLOCK
HOLD = 2


def parity(value, shift):
    while shift:
        value = value ^ (value >> shift)
        shift //= 2
    return value & 1


def sign_of(odd):
    return (1 - 2 * odd).astype(jnp.float32)


def mixed_chunk(position, rows, x_ref):
    count = rows.shape[1]
    bit = lambda k: sign_of((rows >> k) & 1)
    wide = lambda k: jnp.broadcast_to(bit(k), (16, count)).astype(jnp.bfloat16)
    spread = jnp.broadcast_to(rows, (16, count))
    low = parity(spread & lax.broadcasted_iota(jnp.int32, (16, count), 0), 2)
    tiles = [sign_of(low).astype(jnp.bfloat16)]
    for k in range(4, 8):
        flip = wide(k)
        tiles = tiles + [tile * flip for tile in tiles]
    upper = [None]
    for k in range(8, 11):
        flip = wide(k)
        upper = upper + [flip if one is None else one * flip for one in upper]
    total = jnp.zeros((SPLIT * COLS, count), jnp.float32)
    for k, flip in enumerate(upper):
        signs = jnp.concatenate([tile if flip is None else tile * flip for tile in tiles], axis=0)
        total = total + jnp.dot(
            x_ref[:, k * 256:(k + 1) * 256], signs, preferred_element_type=jnp.float32
        )
    parts = [total[a * COLS:(a + 1) * COLS] for a in range(SPLIT)]
    for k in (11, 12):
        flip = bit(k)
        parts = [parts[2 * i] + flip * parts[2 * i + 1] for i in range(len(parts) // 2)]
    weight = sign_of(parity((rows >> 13) & position, 4)) * (1.0 / 1024.0)
    return parts[0] * weight


def kernel(
    x_ref, sign_ref, rows_ref, sketch_ref, gram_ref,
    xs, part, got_core, summed, got_first, middle, got_second, got_plane, send_z, got_z,
    both, gram_part, got_rs, totals, pieces,
    core_send, core_recv, first_send, first_recv, second_send, second_recv,
    plane_send, plane_recv, z_send, z_recv,
    col_sem, rs_send, rs_recv, tot_send, tot_recv, out_send, out_recv,
):
    position = lax.axis_index("row")
    col = lax.axis_index("col")
    z = position // 16
    y = (position // 8) % 2
    x = (position // 2) % 4
    core = position % 2
    mine = y * 4 + x

    def device(z_at=z, y_at=y, x_at=x, core_at=core):
        return (((z_at * 2 + y_at) * 4 + x_at) * 2 + core_at, col)

    def in_plane(d):
        return device(y_at=y ^ (d // 4), x_at=x ^ (d % 4))

    def in_line(d):
        return device(x_at=x ^ (d // 2), core_at=core ^ (d % 2))

    def across(k):
        other = (z * 2 + y + k) % 16
        return device(z_at=other // 2, y_at=other % 2)

    partner = (position, 1 - col)

    barrier = pltpu.get_barrier_semaphore()
    known = [in_plane(d) for d in range(1, 8)]
    known += [in_line(d) for d in (1, 3, 5, 7)]
    known += [device(z_at=(z + k) % Z, y_at=y ^ d) for k in range(1, Z) for d in range(2)]
    known += [partner]
    for to in known:
        pl.semaphore_signal(barrier, inc=1, device_id=to, device_id_type=MESH)

    for a in range(SPLIT):
        window = slice(a * DEPTH, (a + 1) * DEPTH)
        xs[a * COLS:(a + 1) * COLS, :] = (
            x_ref[:, window].astype(jnp.float32) * sign_ref[:, window].astype(jnp.float32)
        ).astype(jnp.bfloat16)

    def copy(src, dst, send, recv, to):
        return pltpu.make_async_remote_copy(
            src_ref=src, dst_ref=dst, send_sem=send, recv_sem=recv,
            device_id=to, device_id_type=MESH,
        )

    def target(t):
        return (z + jnp.where(t % 2 == 0, 4 + t // 2, 4 - (t + 1) // 2)) % Z

    def core_copy(t):
        return copy(
            part.at[t, 1 - core], got_core.at[t], core_send.at[t], core_recv.at[t],
            device(core_at=1 - core),
        )

    def x_first(t, d):
        return copy(
            summed.at[t, pl.ds(2 * (x ^ d), 2)], got_first.at[t, pl.ds(2 * (d - 1), 2)],
            first_send.at[t, d - 1], first_recv.at[t, d - 1], device(x_at=x ^ d),
        )

    def y_second(t):
        return copy(
            middle.at[t, 1 - y], got_second.at[t, 0],
            second_send.at[t, 0], second_recv.at[t, 0], device(y_at=1 - y),
        )

    def y_first(t):
        return copy(
            summed.at[t, pl.ds(4 * (1 - y), 4)], got_first.at[t, pl.ds(0, 4)],
            first_send.at[t, 0], first_recv.at[t, 0], device(y_at=1 - y),
        )

    def x_second(t, d):
        return copy(
            middle.at[t, x ^ d], got_second.at[t, d - 1],
            second_send.at[t, d - 1], second_recv.at[t, d - 1], device(x_at=x ^ d),
        )

    def plane_copy(d):
        return copy(
            summed.at[Z - 1, mine ^ d], got_plane.at[d - 1],
            plane_send.at[d - 1], plane_recv.at[d - 1], in_plane(d),
        )

    def z_copy(t):
        return copy(
            send_z.at[t], got_z.at[t], z_send.at[t], z_recv.at[t], device(z_at=target(t))
        )

    def first_stage(t):
        core_copy(t).wait_recv()

        @pl.when(core == 0)
        def _():
            for j in range(PLANE):
                summed[t, (j % 4) * 2 + j // 4] = part[t, 0, j] + got_core[t, j]
            for d in (2, 1, 3):
                x_first(t, d).start()

        @pl.when(core == 1)
        def _():
            for j in range(PLANE):
                summed[t, j] = part[t, 1, j] + got_core[t, j]
            y_first(t).start()

    def second_stage(t):
        @pl.when(core == 0)
        def _():
            for d in range(1, 4):
                x_first(t, d).wait_recv()
            for j in range(2):
                middle[t, j] = (
                    (summed[t, 2 * x + j] + got_first[t, j])
                    + (got_first[t, 2 + j] + got_first[t, 4 + j])
                )
            y_second(t).start()

        @pl.when(core == 1)
        def _():
            y_first(t).wait_recv()
            for j in range(4):
                middle[t, j] = summed[t, 4 * y + j] + got_first[t, j]
            for d in (2, 1, 3):
                x_second(t, d).start()

    def third_stage(t):
        @pl.when(core == 0)
        def _():
            y_second(t).wait_recv()
            send_z[t] = middle[t, y] + got_second[t, 0]

        @pl.when(core == 1)
        def _():
            for d in range(1, 4):
                x_second(t, d).wait_recv()
            send_z[t] = (middle[t, x] + got_second[t, 0]) + (got_second[t, 1] + got_second[t, 2])

        z_copy(t).start()

    def step(t, carry):
        start = pl.multiple_of(target(t) * CHUNK, CHUNK)
        chunk = mixed_chunk(position, rows_ref[:, pl.ds(start, CHUNK)], xs)
        for j in range(16):
            part[t, j % 2, j // 2] = chunk[:, j * BLOCK:(j + 1) * BLOCK]

        @pl.when(t == HOLD - 1)
        def _():
            pl.semaphore_wait(barrier, len(known))
            for k in range(HOLD):
                core_copy(k).start()

        @pl.when(t >= HOLD)
        def _():
            core_copy(t).start()

        @pl.when(t == HOLD)
        def _():
            for k in range(HOLD):
                first_stage(k)

        @pl.when(t > HOLD)
        def _():
            first_stage(t - 1)

        @pl.when(t == HOLD + 2)
        def _():
            for k in range(HOLD):
                second_stage(k)

        @pl.when(t > HOLD + 2)
        def _():
            second_stage(t - 3)

        @pl.when(t == Z - 1)
        def _():
            for k in range(HOLD):
                third_stage(k)

        return carry

    lax.fori_loop(0, Z, step, 0)

    last = Z - 1
    core_copy(last).wait_recv()
    summed[last] = part[last, core] + got_core[last]
    for d in (6, 7, 5, 2, 3, 1, 4):
        plane_copy(d).start()
    for k in range(last - 2, last):
        second_stage(k)
    for k in range(HOLD, last):
        third_stage(k)

    for d in range(1, PLANE):
        plane_copy(d).wait_recv()
    own = summed[last, mine]
    for d in range(1, PLANE):
        own = own + got_plane[d - 1]
    for t in range(last):
        z_copy(t).wait_recv()
        own = own + got_z[t]
    sketch_ref[...] = own

    def place(at):
        return pl.ds(pl.multiple_of(at * COLS, COLS), COLS)

    both[place(col), :] = own

    def col_copy(at):
        return copy(both.at[place(at)], both.at[place(at)], col_sem.at[0], col_sem.at[1], partner)

    col_copy(col).start()
    col_copy(1 - col).wait_recv()
    gram_part[...] = lax.dot_general(
        own, both[...], (((1,), (1,)), ((), ())),
        precision=lax.Precision.HIGHEST, preferred_element_type=jnp.float32,
    ).reshape(PLANE, 8, 128)

    line = x * 2 + core

    def rs_copy(d):
        return copy(
            gram_part.at[line ^ d], got_rs.at[d - 1], rs_send.at[d - 1], rs_recv.at[d - 1], in_line(d)
        )

    for d in (4, 5, 2, 3, 6, 7, 1):
        rs_copy(d).start()
    for d in range(1, PLANE):
        rs_copy(d).wait_recv()
    piece = gram_part[line]
    for d in range(1, PLANE):
        piece = piece + got_rs[d - 1]
    me = z * 2 + y
    totals[me] = piece

    def tot_copy(k, at):
        return copy(totals.at[at], totals.at[at], tot_send.at[k - 1], tot_recv.at[k - 1], across(k))

    for k in (8, 7, 9, 6, 10, 5, 11, 4, 12, 3, 13, 2, 14, 1, 15):
        tot_copy(k, me).start()
    for k in range(1, 16):
        tot_copy(k, (me + 16 - k) % 16).wait_recv()
    piece = totals[0]
    for k in range(1, 16):
        piece = piece + totals[k]
    pieces[line] = piece * (1.0 / 16384.0)

    def out_copy(d, at):
        return copy(pieces.at[at], pieces.at[at], out_send.at[d - 1], out_recv.at[d - 1], in_line(d))

    for d in (4, 5, 2, 3, 6, 7, 1):
        out_copy(d, line).start()
    for d in range(1, PLANE):
        out_copy(d, line ^ d).wait_recv()
    gram_ref[...] = pieces[...].reshape(COLS, 128)

    def drain(t, carry):
        core_copy(t).wait_send()
        return carry

    def drain_stages(t, carry):
        @pl.when(core == 0)
        def _():
            for d in range(1, 4):
                x_first(t, d).wait_send()
            y_second(t).wait_send()

        @pl.when(core == 1)
        def _():
            y_first(t).wait_send()
            for d in range(1, 4):
                x_second(t, d).wait_send()

        z_copy(t).wait_send()
        return carry

    lax.fori_loop(0, Z, drain, 0)
    lax.fori_loop(0, last, drain_stages, 0)
    col_copy(col).wait_send()
    for d in range(1, PLANE):
        plane_copy(d).wait_send()
        rs_copy(d).wait_send()
        out_copy(d, line).wait_send()
    for k in range(1, 16):
        tot_copy(k, me).wait_send()


def hand_over(sketch_ref, gram_ref, sketch_out, gram_out):
    sketch_out[...] = sketch_ref[...]
    gram_out[...] = gram_ref[...]


def body(matrix_panel, row_signs, sample_rows):
    vmem = pl.BlockSpec(memory_space=pltpu.VMEM)
    f32 = jnp.float32
    block = (COLS, BLOCK)
    sems = pltpu.SemaphoreType.DMA
    outs = (jax.ShapeDtypeStruct(block, f32), jax.ShapeDtypeStruct(block, f32))
    sketch, gram = pl.pallas_call(
        kernel,
        out_shape=outs,
        in_specs=[vmem] * 3,
        out_specs=(vmem, vmem),
        scratch_shapes=[
            pltpu.VMEM((SPLIT * COLS, DEPTH), jnp.bfloat16),
            pltpu.VMEM((Z, CORES, PLANE) + block, f32),
            pltpu.VMEM((Z, PLANE) + block, f32),
            pltpu.VMEM((Z, PLANE) + block, f32),
            pltpu.VMEM((Z - 1, 6) + block, f32),
            pltpu.VMEM((Z - 1, 4) + block, f32),
            pltpu.VMEM((Z - 1, 3) + block, f32),
            pltpu.VMEM((PLANE - 1,) + block, f32),
            pltpu.VMEM((Z - 1,) + block, f32),
            pltpu.VMEM((Z - 1,) + block, f32),
            pltpu.VMEM((2 * COLS, BLOCK), f32),
            pltpu.VMEM((PLANE, 8, 128), f32),
            pltpu.VMEM((PLANE - 1, 8, 128), f32),
            pltpu.VMEM((16, 8, 128), f32),
            pltpu.VMEM((PLANE, 8, 128), f32),
            sems((Z,)), sems((Z,)),
            sems((Z - 1, 3)), sems((Z - 1, 3)),
            sems((Z - 1, 3)), sems((Z - 1, 3)),
            sems((PLANE - 1,)), sems((PLANE - 1,)),
            sems((Z - 1,)), sems((Z - 1,)),
            sems((2,)),
            sems((PLANE - 1,)), sems((PLANE - 1,)),
            sems((15,)), sems((15,)),
            sems((PLANE - 1,)), sems((PLANE - 1,)),
        ],
        compiler_params=pltpu.CompilerParams(
            collective_id=0, has_side_effects=True, vmem_limit_bytes=56 * 2**20
        ),
        cost_estimate=pl.CostEstimate(
            flops=2 * COLS * 8192 * 16384, bytes_accessed=2**21, transcendentals=0
        ),
    )(matrix_panel, row_signs.reshape(1, -1), sample_rows.reshape(1, -1))
    return pl.pallas_call(
        hand_over, out_shape=outs, in_specs=[vmem] * 2, out_specs=(vmem, vmem)
    )(sketch, gram)


def solution(mesh):
    return jax.shard_map(
        body,
        mesh=mesh,
        in_specs=(P("col", "row"), P("row"), P()),
        out_specs=(P("col", "row"), P("col", None)),
        check_vma=False,
    )
```

```python
import functools

import jax
import jax.numpy as jnp
from jax import lax
from jax.experimental import pallas as pl
from jax.experimental.pallas import tpu as pltpu
from jax.sharding import PartitionSpec as P

MESH = pl.DeviceIdType.MESH
Z = 8
PLANE = 8
CORES = 2
BLOCK = 128
COLS = 64
SPLIT = 4
DEPTH = 2048
CHUNK = PLANE * CORES * BLOCK
TWO_STEP = 6


def parity(value, shift):
    while shift:
        value = value ^ (value >> shift)
        shift //= 2
    return value & 1


def sign_of(odd):
    return (1 - 2 * odd).astype(jnp.float32)


def mixed_chunk(position, rows, x_ref):
    count = rows.shape[1]
    bit = lambda k: sign_of((rows >> k) & 1)
    wide = lambda k: jnp.broadcast_to(bit(k), (16, count)).astype(jnp.bfloat16)
    spread = jnp.broadcast_to(rows, (16, count))
    low = parity(spread & lax.broadcasted_iota(jnp.int32, (16, count), 0), 2)
    tiles = [sign_of(low).astype(jnp.bfloat16)]
    for k in range(4, 8):
        flip = wide(k)
        tiles = tiles + [tile * flip for tile in tiles]
    upper = [None]
    for k in range(8, 11):
        flip = wide(k)
        upper = upper + [flip if one is None else one * flip for one in upper]
    total = jnp.zeros((SPLIT * COLS, count), jnp.float32)
    for k, flip in enumerate(upper):
        signs = jnp.concatenate([tile if flip is None else tile * flip for tile in tiles], axis=0)
        total = total + jnp.dot(
            x_ref[:, k * 256:(k + 1) * 256], signs, preferred_element_type=jnp.float32
        )
    parts = [total[a * COLS:(a + 1) * COLS] for a in range(SPLIT)]
    for k in (11, 12):
        flip = bit(k)
        parts = [parts[2 * i] + flip * parts[2 * i + 1] for i in range(len(parts) // 2)]
    weight = sign_of(parity((rows >> 13) & position, 4)) * (1.0 / 1024.0)
    return parts[0] * weight


def kernel(
    x_ref, sign_ref, rows_ref, sketch_ref, gram_ref,
    xs, part, got_core, summed, got_first, middle, got_second, got_plane, send_z, got_z,
    got_cross, early, got_early, both, gram_part, got_rs, totals, pieces,
    greet, core_send, core_recv, first_send, first_recv, second_send, second_recv,
    plane_send, plane_recv, z_send, z_recv,
    cross_sem, col_sem, rs_send, rs_recv, tot_send, tot_recv, out_send, out_recv,
):
    position = lax.axis_index("row")
    col = lax.axis_index("col")
    z = position // 16
    y = (position // 8) % 2
    x = (position // 2) % 4
    core = position % 2
    mine = y * 4 + x

    def device(z_at=z, y_at=y, x_at=x, core_at=core, col_at=col):
        return (((z_at * 2 + y_at) * 4 + x_at) * 2 + core_at, col_at)

    def in_plane(d):
        return device(y_at=y ^ (d // 4), x_at=x ^ (d % 4))

    def in_line(d):
        return device(x_at=x ^ (d // 2), core_at=core ^ (d % 2))

    def across(k):
        other = (z * 2 + y + k) % 16
        return device(z_at=other // 2, y_at=other % 2)

    partner = (position, 1 - col)

    barrier = pltpu.get_barrier_semaphore()
    beside = [device(z_at=(z + 1) % Z), device(z_at=(z + 7) % Z)]
    known = beside + [in_plane(d) for d in range(1, 8)]
    known += [in_line(d) for d in (1, 3, 5, 7)]
    known += [partner]
    for to in known:
        pl.semaphore_signal(barrier, inc=1, device_id=to, device_id_type=MESH)

    for a in range(SPLIT):
        window = slice(a * DEPTH, (a + 1) * DEPTH)
        xs[a * COLS:(a + 1) * COLS, :] = (
            x_ref[:, window].astype(jnp.float32) * sign_ref[:, window].astype(jnp.float32)
        ).astype(jnp.bfloat16)

    def copy(src, dst, send, recv, to):
        return pltpu.make_async_remote_copy(
            src_ref=src, dst_ref=dst, send_sem=send, recv_sem=recv,
            device_id=to, device_id_type=MESH,
        )

    def target(t):
        return (z + jnp.where(t % 2 == 0, 4 + t // 2, 4 - (t + 1) // 2)) % Z

    def core_copy(t):
        return copy(
            part.at[t, 1 - core], got_core.at[t], core_send.at[t], core_recv.at[t],
            device(core_at=1 - core),
        )

    def x_first(t, d):
        return copy(
            summed.at[t, pl.ds(2 * (x ^ d), 2)], got_first.at[t, pl.ds(2 * (d - 1), 2)],
            first_send.at[t, d - 1], first_recv.at[t, d - 1], device(x_at=x ^ d),
        )

    def y_second(t):
        return copy(
            middle.at[t, 1 - y], got_second.at[t, 0],
            second_send.at[t, 0], second_recv.at[t, 0], device(y_at=1 - y),
        )

    def y_first(t):
        return copy(
            summed.at[t, pl.ds(4 * (1 - y), 4)], got_first.at[t, pl.ds(0, 4)],
            first_send.at[t, 0], first_recv.at[t, 0], device(y_at=1 - y),
        )

    def x_second(t, d):
        return copy(
            middle.at[t, x ^ d], got_second.at[t, d - 1],
            second_send.at[t, d - 1], second_recv.at[t, d - 1], device(x_at=x ^ d),
        )

    def plane_copy(t, d):
        return copy(
            summed.at[t, mine ^ d], got_plane.at[t - TWO_STEP, d - 1],
            plane_send.at[t - TWO_STEP, d - 1], plane_recv.at[t - TWO_STEP, d - 1], in_plane(d),
        )

    def cross_copy():
        return copy(
            send_z.at[Z - 2], got_cross, cross_sem.at[0], cross_sem.at[1],
            device(z_at=(z + 7) % Z, col_at=1 - col),
        )

    def z_copy(t):
        return copy(
            send_z.at[t], got_z.at[t], z_send.at[t], z_recv.at[t], device(z_at=target(t))
        )

    def first_stage(t):
        core_copy(t).wait_recv()

        @pl.when(core == 0)
        def _():
            for j in range(PLANE):
                summed[t, (j % 4) * 2 + j // 4] = part[t, 0, j] + got_core[t, j]
            for d in (2, 1, 3):
                x_first(t, d).start()

        @pl.when(core == 1)
        def _():
            for j in range(PLANE):
                summed[t, j] = part[t, 1, j] + got_core[t, j]
            y_first(t).start()

    def second_stage(t):
        @pl.when(core == 0)
        def _():
            for d in range(1, 4):
                x_first(t, d).wait_recv()
            for j in range(2):
                middle[t, j] = (
                    (summed[t, 2 * x + j] + got_first[t, j])
                    + (got_first[t, 2 + j] + got_first[t, 4 + j])
                )
            y_second(t).start()

        @pl.when(core == 1)
        def _():
            y_first(t).wait_recv()
            for j in range(4):
                middle[t, j] = summed[t, 4 * y + j] + got_first[t, j]
            for d in (2, 1, 3):
                x_second(t, d).start()

    def third_stage(t):
        @pl.when(core == 0)
        def _():
            y_second(t).wait_recv()
            send_z[t] = middle[t, y] + got_second[t, 0]

        @pl.when(core == 1)
        def _():
            for d in range(1, 4):
                x_second(t, d).wait_recv()
            send_z[t] = (middle[t, x] + got_second[t, 0]) + (got_second[t, 1] + got_second[t, 2])

        z_copy(t).start()

    def plane_stage(t):
        core_copy(t).wait_recv()
        summed[t] = part[t, core] + got_core[t]
        for d in (6, 7, 5, 2, 3, 1, 4):
            plane_copy(t, d).start()

    def plane_sum(t):
        for d in range(1, PLANE):
            plane_copy(t, d).wait_recv()
        block = summed[t, mine]
        for d in range(1, PLANE):
            block = block + got_plane[t - TWO_STEP, d - 1]
        return block

    def each(stage, first, end):
        def one(k, carry):
            stage(k)
            return carry

        lax.fori_loop(first, end, one, 0)

    last = Z - 1
    hold = jnp.where(z < 3, 2, 1)

    def step(t, carry):
        start = pl.multiple_of(target(t) * CHUNK, CHUNK)
        chunk = mixed_chunk(position, rows_ref[:, pl.ds(start, CHUNK)], xs)
        for j in range(16):
            part[t, j % 2, j // 2] = chunk[:, j * BLOCK:(j + 1) * BLOCK]

        @pl.when(t == hold - 1)
        def _():
            pl.semaphore_wait(barrier, len(known))
            each(lambda k: core_copy(k).start(), 0, hold)

        @pl.when(t >= hold)
        def _():
            core_copy(t).start()

        @pl.when((t >= hold) & (t < hold + 3))
        def _():
            pl.semaphore_wait(greet.at[t - hold], 2)

        @pl.when((t >= hold - 1) & (t < hold + 2))
        def _():
            for to in beside:
                pl.semaphore_signal(greet.at[t - hold + 1], inc=1, device_id=to, device_id_type=MESH)

        @pl.when((t >= hold) & (t < last))
        def _():
            each(first_stage, jnp.where(t == hold, 0, t - 1), t)

        @pl.when(t == last)
        def _():
            plane_stage(last - 1)

        @pl.when(t >= 5)
        def _():
            each(second_stage, 2 * (t - 5), jnp.minimum(2 * (t - 5) + 2, 5))

        @pl.when(t == last)
        def _():
            each(third_stage, 0, 2)

        return carry

    lax.fori_loop(0, Z, step, 0)

    plane_stage(last)
    second_stage(5)
    each(third_stage, 2, TWO_STEP)
    send_z[last - 1] = plane_sum(last - 1)
    z_copy(last - 1).start()
    cross_copy().start()
    own = plane_sum(last)
    for t in range(last - 1):
        z_copy(t).wait_recv()
        own = own + got_z[t]
    early[...] = own

    def place(at):
        return pl.ds(pl.multiple_of(at * COLS, COLS), COLS)

    def col_copy():
        return copy(early, got_early, col_sem.at[0], col_sem.at[1], partner)

    col_copy().start()
    z_copy(last - 1).wait_recv()
    own = own + got_z[last - 1]
    sketch_ref[...] = own
    both[place(col), :] = own
    cross_copy().wait_recv()
    col_copy().wait_recv()
    both[place(1 - col), :] = got_early[...] + got_cross[...]
    gram_part[...] = lax.dot_general(
        own, both[...], (((1,), (1,)), ((), ())),
        precision=lax.Precision.HIGHEST, preferred_element_type=jnp.float32,
    ).reshape(PLANE, 8, 128)

    line = x * 2 + core

    def rs_copy(d):
        return copy(
            gram_part.at[line ^ d], got_rs.at[d - 1], rs_send.at[d - 1], rs_recv.at[d - 1], in_line(d)
        )

    for d in (4, 5, 2, 3, 6, 7, 1):
        rs_copy(d).start()
    for d in range(1, PLANE):
        rs_copy(d).wait_recv()
    piece = gram_part[line]
    for d in range(1, PLANE):
        piece = piece + got_rs[d - 1]
    me = z * 2 + y
    totals[me] = piece

    def tot_copy(k, at):
        return copy(totals.at[at], totals.at[at], tot_send.at[k - 1], tot_recv.at[k - 1], across(k))

    for k in (8, 7, 9, 6, 10, 5, 11, 4, 12, 3, 13, 2, 14, 1, 15):
        tot_copy(k, me).start()
    for k in range(1, 16):
        tot_copy(k, (me + 16 - k) % 16).wait_recv()
    piece = totals[0]
    for k in range(1, 16):
        piece = piece + totals[k]
    pieces[line] = piece * (1.0 / 16384.0)

    def out_copy(d, at):
        return copy(pieces.at[at], pieces.at[at], out_send.at[d - 1], out_recv.at[d - 1], in_line(d))

    for d in (4, 5, 2, 3, 6, 7, 1):
        out_copy(d, line).start()
    for d in range(1, PLANE):
        out_copy(d, line ^ d).wait_recv()
    gram_ref[...] = pieces[...].reshape(COLS, 128)

    def drain(t, carry):
        core_copy(t).wait_send()
        return carry

    def drain_stages(t, carry):
        @pl.when(core == 0)
        def _():
            for d in range(1, 4):
                x_first(t, d).wait_send()
            y_second(t).wait_send()

        @pl.when(core == 1)
        def _():
            y_first(t).wait_send()
            for d in range(1, 4):
                x_second(t, d).wait_send()

        z_copy(t).wait_send()
        return carry

    lax.fori_loop(0, Z, drain, 0)
    lax.fori_loop(0, TWO_STEP, drain_stages, 0)
    z_copy(last - 1).wait_send()
    cross_copy().wait_send()
    col_copy().wait_send()
    for d in range(1, PLANE):
        plane_copy(last - 1, d).wait_send()
        plane_copy(last, d).wait_send()
        rs_copy(d).wait_send()
        out_copy(d, line).wait_send()
    for k in range(1, 16):
        tot_copy(k, me).wait_send()


def hand_over(sketch_ref, gram_ref, sketch_out, gram_out):
    sketch_out[...] = sketch_ref[...]
    gram_out[...] = gram_ref[...]


def body(matrix_panel, row_signs, sample_rows):
    vmem = pl.BlockSpec(memory_space=pltpu.VMEM)
    f32 = jnp.float32
    block = (COLS, BLOCK)
    sems = pltpu.SemaphoreType.DMA
    outs = (jax.ShapeDtypeStruct(block, f32), jax.ShapeDtypeStruct(block, f32))
    sketch, gram = pl.pallas_call(
        kernel,
        out_shape=outs,
        in_specs=[vmem] * 3,
        out_specs=(vmem, vmem),
        scratch_shapes=[
            pltpu.VMEM((SPLIT * COLS, DEPTH), jnp.bfloat16),
            pltpu.VMEM((Z, CORES, PLANE) + block, f32),
            pltpu.VMEM((Z, PLANE) + block, f32),
            pltpu.VMEM((Z, PLANE) + block, f32),
            pltpu.VMEM((TWO_STEP, 6) + block, f32),
            pltpu.VMEM((TWO_STEP, 4) + block, f32),
            pltpu.VMEM((TWO_STEP, 3) + block, f32),
            pltpu.VMEM((Z - TWO_STEP, PLANE - 1) + block, f32),
            pltpu.VMEM((Z - 1,) + block, f32),
            pltpu.VMEM((Z - 1,) + block, f32),
            pltpu.VMEM(block, f32),
            pltpu.VMEM(block, f32),
            pltpu.VMEM(block, f32),
            pltpu.VMEM((2 * COLS, BLOCK), f32),
            pltpu.VMEM((PLANE, 8, 128), f32),
            pltpu.VMEM((PLANE - 1, 8, 128), f32),
            pltpu.VMEM((16, 8, 128), f32),
            pltpu.VMEM((PLANE, 8, 128), f32),
            pltpu.SemaphoreType.REGULAR((3,)),
            sems((Z,)), sems((Z,)),
            sems((TWO_STEP, 3)), sems((TWO_STEP, 3)),
            sems((TWO_STEP, 3)), sems((TWO_STEP, 3)),
            sems((Z - TWO_STEP, PLANE - 1)), sems((Z - TWO_STEP, PLANE - 1)),
            sems((Z - 1,)), sems((Z - 1,)),
            sems((2,)), sems((2,)),
            sems((PLANE - 1,)), sems((PLANE - 1,)),
            sems((15,)), sems((15,)),
            sems((PLANE - 1,)), sems((PLANE - 1,)),
        ],
        compiler_params=pltpu.CompilerParams(
            collective_id=0, has_side_effects=True, vmem_limit_bytes=56 * 2**20
        ),
        cost_estimate=pl.CostEstimate(
            flops=2 * COLS * 8192 * 16384, bytes_accessed=2**21, transcendentals=0
        ),
    )(matrix_panel, row_signs.reshape(1, -1), sample_rows.reshape(1, -1))
    return pl.pallas_call(
        hand_over, out_shape=outs, in_specs=[vmem] * 2, out_specs=(vmem, vmem)
    )(sketch, gram)


def solution(mesh):
    return jax.shard_map(
        body,
        mesh=mesh,
        in_specs=(P("col", "row"), P("row"), P()),
        out_specs=(P("col", "row"), P("col", None)),
        check_vma=False,
    )
```

```python
import functools

import jax
import jax.numpy as jnp
from jax import lax
from jax.experimental import pallas as pl
from jax.experimental.pallas import tpu as pltpu
from jax.sharding import PartitionSpec as P

MESH = pl.DeviceIdType.MESH
Z = 8
PLANE = 8
CORES = 2
BLOCK = 128
COLS = 64
SPLIT = 4
DEPTH = 2048
CHUNK = PLANE * CORES * BLOCK
TWO_STEP = 5


def parity(value, shift):
    while shift:
        value = value ^ (value >> shift)
        shift //= 2
    return value & 1


def sign_of(odd):
    return (1 - 2 * odd).astype(jnp.float32)


def mixed_chunk(position, rows, x_ref):
    count = rows.shape[1]
    bit = lambda k: sign_of((rows >> k) & 1)
    wide = lambda k: jnp.broadcast_to(bit(k), (16, count)).astype(jnp.bfloat16)
    spread = jnp.broadcast_to(rows, (16, count))
    low = parity(spread & lax.broadcasted_iota(jnp.int32, (16, count), 0), 2)
    tiles = [sign_of(low).astype(jnp.bfloat16)]
    for k in range(4, 8):
        flip = wide(k)
        tiles = tiles + [tile * flip for tile in tiles]
    upper = [None]
    for k in range(8, 11):
        flip = wide(k)
        upper = upper + [flip if one is None else one * flip for one in upper]
    total = jnp.zeros((SPLIT * COLS, count), jnp.float32)
    for k, flip in enumerate(upper):
        signs = jnp.concatenate([tile if flip is None else tile * flip for tile in tiles], axis=0)
        total = total + jnp.dot(
            x_ref[:, k * 256:(k + 1) * 256], signs, preferred_element_type=jnp.float32
        )
    parts = [total[a * COLS:(a + 1) * COLS] for a in range(SPLIT)]
    for k in (11, 12):
        flip = bit(k)
        parts = [parts[2 * i] + flip * parts[2 * i + 1] for i in range(len(parts) // 2)]
    weight = sign_of(parity((rows >> 13) & position, 4)) * (1.0 / 1024.0)
    return parts[0] * weight


def kernel(
    x_ref, sign_ref, rows_ref, sketch_ref, gram_ref,
    xs, part, got_core, summed, got_first, middle, got_second, got_plane, send_z, got_z,
    got_cross, early, got_early, both, gram_part, got_rs, totals, pieces,
    greet, core_send, core_recv, first_send, first_recv, second_send, second_recv,
    plane_send, plane_recv, z_send, z_recv,
    cross_sem, col_sem, rs_send, rs_recv, tot_send, tot_recv, out_send, out_recv,
):
    position = lax.axis_index("row")
    col = lax.axis_index("col")
    z = position // 16
    y = (position // 8) % 2
    x = (position // 2) % 4
    core = position % 2
    mine = y * 4 + x

    def device(z_at=z, y_at=y, x_at=x, core_at=core, col_at=col):
        return (((z_at * 2 + y_at) * 4 + x_at) * 2 + core_at, col_at)

    def in_plane(d):
        return device(y_at=y ^ (d // 4), x_at=x ^ (d % 4))

    def in_line(d):
        return device(x_at=x ^ (d // 2), core_at=core ^ (d % 2))

    def across(k):
        other = (z * 2 + y + k) % 16
        return device(z_at=other // 2, y_at=other % 2)

    partner = (position, 1 - col)

    barrier = pltpu.get_barrier_semaphore()
    beside = [device(z_at=(z + 1) % Z), device(z_at=(z + 7) % Z)]
    known = beside + [in_plane(d) for d in range(1, 8)]
    known += [in_line(d) for d in (1, 3, 5, 7)]
    known += [partner]
    for to in known:
        pl.semaphore_signal(barrier, inc=1, device_id=to, device_id_type=MESH)

    for a in range(SPLIT):
        window = slice(a * DEPTH, (a + 1) * DEPTH)
        xs[a * COLS:(a + 1) * COLS, :] = (
            x_ref[:, window].astype(jnp.float32) * sign_ref[:, window].astype(jnp.float32)
        ).astype(jnp.bfloat16)

    def copy(src, dst, send, recv, to):
        return pltpu.make_async_remote_copy(
            src_ref=src, dst_ref=dst, send_sem=send, recv_sem=recv,
            device_id=to, device_id_type=MESH,
        )

    def target(t):
        return (z + jnp.where(t % 2 == 0, 4 + t // 2, 4 - (t + 1) // 2)) % Z

    def core_copy(t):
        return copy(
            part.at[t, 1 - core], got_core.at[t], core_send.at[t], core_recv.at[t],
            device(core_at=1 - core),
        )

    def half_copy(half):
        blocks = pl.ds(4 * half, 4)
        return copy(
            part.at[Z - 1, 1 - core, blocks], got_core.at[Z - 1, blocks],
            core_send.at[Z - 1 + half], core_recv.at[Z - 1 + half], device(core_at=1 - core),
        )

    def x_first(t, d):
        return copy(
            summed.at[t, pl.ds(2 * (x ^ d), 2)], got_first.at[t, pl.ds(2 * (d - 1), 2)],
            first_send.at[t, d - 1], first_recv.at[t, d - 1], device(x_at=x ^ d),
        )

    def y_second(t):
        return copy(
            middle.at[t, 1 - y], got_second.at[t, 0],
            second_send.at[t, 0], second_recv.at[t, 0], device(y_at=1 - y),
        )

    def y_first(t):
        return copy(
            summed.at[t, pl.ds(4 * (1 - y), 4)], got_first.at[t, pl.ds(0, 4)],
            first_send.at[t, 0], first_recv.at[t, 0], device(y_at=1 - y),
        )

    def x_second(t, d):
        return copy(
            middle.at[t, x ^ d], got_second.at[t, d - 1],
            second_send.at[t, d - 1], second_recv.at[t, d - 1], device(x_at=x ^ d),
        )

    def plane_copy(t, d):
        return copy(
            summed.at[t, mine ^ d], got_plane.at[t - TWO_STEP, d - 1],
            plane_send.at[t - TWO_STEP, d - 1], plane_recv.at[t - TWO_STEP, d - 1], in_plane(d),
        )

    def cross_copy():
        return copy(
            send_z.at[Z - 2], got_cross, cross_sem.at[0], cross_sem.at[1],
            device(z_at=(z + 7) % Z, col_at=1 - col),
        )

    def z_copy(t):
        return copy(
            send_z.at[t], got_z.at[t], z_send.at[t], z_recv.at[t], device(z_at=target(t))
        )

    def first_stage(t):
        core_copy(t).wait_recv()

        @pl.when(core == 0)
        def _():
            for j in range(PLANE):
                summed[t, (j % 4) * 2 + j // 4] = part[t, 0, j] + got_core[t, j]
            for d in (2, 1, 3):
                x_first(t, d).start()

        @pl.when(core == 1)
        def _():
            for j in range(PLANE):
                summed[t, j] = part[t, 1, j] + got_core[t, j]
            y_first(t).start()

    def second_stage(t):
        @pl.when(core == 0)
        def _():
            for d in range(1, 4):
                x_first(t, d).wait_recv()
            for j in range(2):
                middle[t, j] = (
                    (summed[t, 2 * x + j] + got_first[t, j])
                    + (got_first[t, 2 + j] + got_first[t, 4 + j])
                )
            y_second(t).start()

        @pl.when(core == 1)
        def _():
            y_first(t).wait_recv()
            for j in range(4):
                middle[t, j] = summed[t, 4 * y + j] + got_first[t, j]
            for d in (2, 1, 3):
                x_second(t, d).start()

    def third_stage(t):
        @pl.when(core == 0)
        def _():
            y_second(t).wait_recv()
            send_z[t] = middle[t, y] + got_second[t, 0]

        @pl.when(core == 1)
        def _():
            for d in range(1, 4):
                x_second(t, d).wait_recv()
            send_z[t] = (middle[t, x] + got_second[t, 0]) + (got_second[t, 1] + got_second[t, 2])

        z_copy(t).start()

    def plane_stage(t):
        core_copy(t).wait_recv()
        summed[t] = part[t, core] + got_core[t]
        for d in (6, 7, 5, 2, 3, 1, 4):
            plane_copy(t, d).start()

    def half_stage(half):
        half_copy(half).wait_recv()
        blocks = pl.ds(4 * half, 4)
        summed[last, blocks] = part[last, core, blocks] + got_core[last, blocks]

        @pl.when(y == half)
        def _():
            for d in (2, 3, 1):
                plane_copy(last, d).start()

        @pl.when(y != half)
        def _():
            for d in (6, 7, 5, 4):
                plane_copy(last, d).start()

    def plane_sum(t):
        for d in range(1, PLANE):
            plane_copy(t, d).wait_recv()
        block = summed[t, mine]
        for d in range(1, PLANE):
            block = block + got_plane[t - TWO_STEP, d - 1]
        return block

    def each(stage, first, end):
        def one(k, carry):
            stage(k)
            return carry

        lax.fori_loop(first, end, one, 0)

    last = Z - 1

    def rows_at(t, begin, count):
        start = pl.multiple_of(target(t) * CHUNK + begin, count)
        return rows_ref[:, pl.ds(start, count)]

    def step(t, carry):
        chunk = mixed_chunk(position, rows_at(t, 0, CHUNK), xs)
        for j in range(16):
            part[t, j % 2, j // 2] = chunk[:, j * BLOCK:(j + 1) * BLOCK]

        @pl.when(t == 0)
        def _():
            pl.semaphore_wait(barrier, len(known))

        core_copy(t).start()

        @pl.when((t >= 1) & (t < 4))
        def _():
            pl.semaphore_wait(greet.at[t - 1], 2)

        @pl.when(t < 3)
        def _():
            for to in beside:
                pl.semaphore_signal(greet.at[t], inc=1, device_id=to, device_id_type=MESH)

        @pl.when((t >= 1) & (t <= TWO_STEP))
        def _():
            first_stage(t - 1)

        @pl.when(t > TWO_STEP)
        def _():
            plane_stage(t - 1)

        @pl.when(t >= 3)
        def _():
            second_stage(t - 3)

        @pl.when(t >= 5)
        def _():
            third_stage(t - 5)

        return carry

    lax.fori_loop(0, last, step, 0)

    for half in range(2):
        chunk = mixed_chunk(position, rows_at(last, half * CHUNK // 2, CHUNK // 2), xs)
        for j in range(8):
            part[last, j % 2, 4 * half + j // 2] = chunk[:, j * BLOCK:(j + 1) * BLOCK]
        half_copy(half).start()
        if half == 0:
            plane_stage(last - 1)
            each(second_stage, 4, TWO_STEP)
            third_stage(2)
        else:
            half_stage(0)
            half_stage(1)

    each(third_stage, 3, TWO_STEP)
    for t in range(TWO_STEP, last):
        send_z[t] = plane_sum(t)
        z_copy(t).start()
    cross_copy().start()
    own = plane_sum(last)
    for t in range(last - 1):
        z_copy(t).wait_recv()
        own = own + got_z[t]
    early[...] = own

    def place(at):
        return pl.ds(pl.multiple_of(at * COLS, COLS), COLS)

    def col_copy():
        return copy(early, got_early, col_sem.at[0], col_sem.at[1], partner)

    col_copy().start()
    z_copy(last - 1).wait_recv()
    own = own + got_z[last - 1]
    sketch_ref[...] = own
    both[place(col), :] = own
    cross_copy().wait_recv()
    col_copy().wait_recv()
    both[place(1 - col), :] = got_early[...] + got_cross[...]
    gram_part[...] = lax.dot_general(
        own, both[...], (((1,), (1,)), ((), ())),
        precision=lax.Precision.HIGHEST, preferred_element_type=jnp.float32,
    ).reshape(PLANE, 8, 128)

    line = x * 2 + core

    def rs_copy(d):
        return copy(
            gram_part.at[line ^ d], got_rs.at[d - 1], rs_send.at[d - 1], rs_recv.at[d - 1], in_line(d)
        )

    for d in (4, 5, 2, 3, 6, 7, 1):
        rs_copy(d).start()
    for d in range(1, PLANE):
        rs_copy(d).wait_recv()
    piece = gram_part[line]
    for d in range(1, PLANE):
        piece = piece + got_rs[d - 1]
    me = z * 2 + y
    totals[me] = piece

    def tot_copy(k, at):
        return copy(totals.at[at], totals.at[at], tot_send.at[k - 1], tot_recv.at[k - 1], across(k))

    for k in (8, 7, 9, 6, 10, 5, 11, 4, 12, 3, 13, 2, 14, 1, 15):
        tot_copy(k, me).start()
    for k in range(1, 16):
        tot_copy(k, (me + 16 - k) % 16).wait_recv()
    piece = totals[0]
    for k in range(1, 16):
        piece = piece + totals[k]
    pieces[line] = piece * (1.0 / 16384.0)

    def out_copy(d, at):
        return copy(pieces.at[at], pieces.at[at], out_send.at[d - 1], out_recv.at[d - 1], in_line(d))

    for d in (4, 5, 2, 3, 6, 7, 1):
        out_copy(d, line).start()
    for d in range(1, PLANE):
        out_copy(d, line ^ d).wait_recv()
    gram_ref[...] = pieces[...].reshape(COLS, 128)

    def drain(t, carry):
        core_copy(t).wait_send()
        return carry

    def drain_stages(t, carry):
        @pl.when(core == 0)
        def _():
            for d in range(1, 4):
                x_first(t, d).wait_send()
            y_second(t).wait_send()

        @pl.when(core == 1)
        def _():
            y_first(t).wait_send()
            for d in range(1, 4):
                x_second(t, d).wait_send()

        z_copy(t).wait_send()
        return carry

    lax.fori_loop(0, last, drain, 0)
    half_copy(0).wait_send()
    half_copy(1).wait_send()
    lax.fori_loop(0, TWO_STEP, drain_stages, 0)
    for t in range(TWO_STEP, last):
        z_copy(t).wait_send()
    cross_copy().wait_send()
    col_copy().wait_send()
    for d in range(1, PLANE):
        for t in range(TWO_STEP, Z):
            plane_copy(t, d).wait_send()
        rs_copy(d).wait_send()
        out_copy(d, line).wait_send()
    for k in range(1, 16):
        tot_copy(k, me).wait_send()


def hand_over(sketch_ref, gram_ref, sketch_out, gram_out):
    sketch_out[...] = sketch_ref[...]
    gram_out[...] = gram_ref[...]


def body(matrix_panel, row_signs, sample_rows):
    vmem = pl.BlockSpec(memory_space=pltpu.VMEM)
    f32 = jnp.float32
    block = (COLS, BLOCK)
    sems = pltpu.SemaphoreType.DMA
    outs = (jax.ShapeDtypeStruct(block, f32), jax.ShapeDtypeStruct(block, f32))
    sketch, gram = pl.pallas_call(
        kernel,
        out_shape=outs,
        in_specs=[vmem] * 3,
        out_specs=(vmem, vmem),
        scratch_shapes=[
            pltpu.VMEM((SPLIT * COLS, DEPTH), jnp.bfloat16),
            pltpu.VMEM((Z, CORES, PLANE) + block, f32),
            pltpu.VMEM((Z, PLANE) + block, f32),
            pltpu.VMEM((Z, PLANE) + block, f32),
            pltpu.VMEM((TWO_STEP, 6) + block, f32),
            pltpu.VMEM((TWO_STEP, 4) + block, f32),
            pltpu.VMEM((TWO_STEP, 3) + block, f32),
            pltpu.VMEM((Z - TWO_STEP, PLANE - 1) + block, f32),
            pltpu.VMEM((Z - 1,) + block, f32),
            pltpu.VMEM((Z - 1,) + block, f32),
            pltpu.VMEM(block, f32),
            pltpu.VMEM(block, f32),
            pltpu.VMEM(block, f32),
            pltpu.VMEM((2 * COLS, BLOCK), f32),
            pltpu.VMEM((PLANE, 8, 128), f32),
            pltpu.VMEM((PLANE - 1, 8, 128), f32),
            pltpu.VMEM((16, 8, 128), f32),
            pltpu.VMEM((PLANE, 8, 128), f32),
            pltpu.SemaphoreType.REGULAR((3,)),
            sems((Z + 1,)), sems((Z + 1,)),
            sems((TWO_STEP, 3)), sems((TWO_STEP, 3)),
            sems((TWO_STEP, 3)), sems((TWO_STEP, 3)),
            sems((Z - TWO_STEP, PLANE - 1)), sems((Z - TWO_STEP, PLANE - 1)),
            sems((Z - 1,)), sems((Z - 1,)),
            sems((2,)), sems((2,)),
            sems((PLANE - 1,)), sems((PLANE - 1,)),
            sems((15,)), sems((15,)),
            sems((PLANE - 1,)), sems((PLANE - 1,)),
        ],
        compiler_params=pltpu.CompilerParams(
            collective_id=0, has_side_effects=True, vmem_limit_bytes=56 * 2**20
        ),
        cost_estimate=pl.CostEstimate(
            flops=2 * COLS * 8192 * 16384, bytes_accessed=2**21, transcendentals=0
        ),
    )(matrix_panel, row_signs.reshape(1, -1), sample_rows.reshape(1, -1))
    return pl.pallas_call(
        hand_over, out_shape=outs, in_specs=[vmem] * 2, out_specs=(vmem, vmem)
    )(sketch, gram)


def solution(mesh):
    return jax.shard_map(
        body,
        mesh=mesh,
        in_specs=(P("col", "row"), P("row"), P()),
        out_specs=(P("col", "row"), P("col", None)),
        check_vma=False,
    )
```

```python
import functools

import jax
import jax.numpy as jnp
from jax import lax
from jax.experimental import pallas as pl
from jax.experimental.pallas import tpu as pltpu
from jax.sharding import PartitionSpec as P

MESH = pl.DeviceIdType.MESH
Z = 8
PLANE = 8
CORES = 2
BLOCK = 128
COLS = 64
SPLIT = 4
DEPTH = 2048
CHUNK = PLANE * CORES * BLOCK
TWO_STEP = 6


def parity(value, shift):
    while shift:
        value = value ^ (value >> shift)
        shift //= 2
    return value & 1


def sign_of(odd):
    return (1 - 2 * odd).astype(jnp.float32)


def mixed_chunk(position, rows, x_ref):
    count = rows.shape[1]
    bit = lambda k: sign_of((rows >> k) & 1)
    wide = lambda k: jnp.broadcast_to(bit(k), (16, count)).astype(jnp.bfloat16)
    spread = jnp.broadcast_to(rows, (16, count))
    low = parity(spread & lax.broadcasted_iota(jnp.int32, (16, count), 0), 2)
    tiles = [sign_of(low).astype(jnp.bfloat16)]
    for k in range(4, 8):
        flip = wide(k)
        tiles = tiles + [tile * flip for tile in tiles]
    upper = [None]
    for k in range(8, 11):
        flip = wide(k)
        upper = upper + [flip if one is None else one * flip for one in upper]
    total = jnp.zeros((SPLIT * COLS, count), jnp.float32)
    for k, flip in enumerate(upper):
        signs = jnp.concatenate([tile if flip is None else tile * flip for tile in tiles], axis=0)
        total = total + jnp.dot(
            x_ref[:, k * 256:(k + 1) * 256], signs, preferred_element_type=jnp.float32
        )
    parts = [total[a * COLS:(a + 1) * COLS] for a in range(SPLIT)]
    for k in (11, 12):
        flip = bit(k)
        parts = [parts[2 * i] + flip * parts[2 * i + 1] for i in range(len(parts) // 2)]
    weight = sign_of(parity((rows >> 13) & position, 4)) * (1.0 / 1024.0)
    return parts[0] * weight


def kernel(
    x_ref, sign_ref, rows_ref, sketch_ref, gram_ref,
    xs, part, got_core, summed, got_first, middle, got_second, got_plane, send_z, got_z,
    got_cross, early, got_early, both, gram_part, got_rs, totals, pieces,
    greet, core_send, core_recv, first_send, first_recv, second_send, second_recv,
    plane_send, plane_recv, z_send, z_recv,
    cross_sem, col_sem, rs_send, rs_recv, tot_send, tot_recv, out_send, out_recv,
):
    position = lax.axis_index("row")
    col = lax.axis_index("col")
    z = position // 16
    y = (position // 8) % 2
    x = (position // 2) % 4
    core = position % 2
    mine = y * 4 + x

    def device(z_at=z, y_at=y, x_at=x, core_at=core, col_at=col):
        return (((z_at * 2 + y_at) * 4 + x_at) * 2 + core_at, col_at)

    def in_plane(d):
        return device(y_at=y ^ (d // 4), x_at=x ^ (d % 4))

    def in_line(d):
        return device(x_at=x ^ (d // 2), core_at=core ^ (d % 2))

    def across(k):
        other = (z * 2 + y + k) % 16
        return device(z_at=other // 2, y_at=other % 2)

    partner = (position, 1 - col)

    barrier = pltpu.get_barrier_semaphore()
    beside = [device(z_at=(z + 1) % Z), device(z_at=(z + 7) % Z)]
    known = beside + [in_plane(d) for d in range(1, 8)]
    known += [in_line(d) for d in (1, 3, 5, 7)]
    known += [partner]
    for to in known:
        pl.semaphore_signal(barrier, inc=1, device_id=to, device_id_type=MESH)

    for a in range(SPLIT):
        window = slice(a * DEPTH, (a + 1) * DEPTH)
        signs = sign_ref[:, window].astype(jnp.float32).astype(jnp.bfloat16)
        xs[a * COLS:(a + 1) * COLS, :] = x_ref[:, window] * signs

    def copy(src, dst, send, recv, to):
        return pltpu.make_async_remote_copy(
            src_ref=src, dst_ref=dst, send_sem=send, recv_sem=recv,
            device_id=to, device_id_type=MESH,
        )

    def target(t):
        return (z + jnp.where(t % 2 == 0, 4 + t // 2, 4 - (t + 1) // 2)) % Z

    def core_copy(t):
        return copy(
            part.at[t, 1 - core], got_core.at[t], core_send.at[t], core_recv.at[t],
            device(core_at=1 - core),
        )

    def half_copy(half):
        blocks = pl.ds(4 * half, 4)
        return copy(
            part.at[Z - 1, 1 - core, blocks], got_core.at[Z - 1, blocks],
            core_send.at[Z - 1 + half], core_recv.at[Z - 1 + half], device(core_at=1 - core),
        )

    def x_first(t, d):
        return copy(
            summed.at[t, pl.ds(2 * (x ^ d), 2)], got_first.at[t, pl.ds(2 * (d - 1), 2)],
            first_send.at[t, d - 1], first_recv.at[t, d - 1], device(x_at=x ^ d),
        )

    def y_second(t):
        return copy(
            middle.at[t, 1 - y], got_second.at[t, 0],
            second_send.at[t, 0], second_recv.at[t, 0], device(y_at=1 - y),
        )

    def y_first(t):
        return copy(
            summed.at[t, pl.ds(4 * (1 - y), 4)], got_first.at[t, pl.ds(0, 4)],
            first_send.at[t, 0], first_recv.at[t, 0], device(y_at=1 - y),
        )

    def x_second(t, d):
        return copy(
            middle.at[t, x ^ d], got_second.at[t, d - 1],
            second_send.at[t, d - 1], second_recv.at[t, d - 1], device(x_at=x ^ d),
        )

    def plane_copy(t, d):
        return copy(
            summed.at[t, mine ^ d], got_plane.at[t - TWO_STEP, d - 1],
            plane_send.at[t - TWO_STEP, d - 1], plane_recv.at[t - TWO_STEP, d - 1], in_plane(d),
        )

    def cross_copy():
        return copy(
            send_z.at[Z - 2], got_cross, cross_sem.at[0], cross_sem.at[1],
            device(z_at=(z + 7) % Z, col_at=1 - col),
        )

    def z_copy(t):
        return copy(
            send_z.at[t], got_z.at[t], z_send.at[t], z_recv.at[t], device(z_at=target(t))
        )

    def first_stage(t):
        core_copy(t).wait_recv()

        @pl.when(core == 0)
        def _():
            for j in range(PLANE):
                summed[t, (j % 4) * 2 + j // 4] = part[t, 0, j] + got_core[t, j]
            for d in (2, 1, 3):
                x_first(t, d).start()

        @pl.when(core == 1)
        def _():
            for j in range(PLANE):
                summed[t, j] = part[t, 1, j] + got_core[t, j]
            y_first(t).start()

    def second_stage(t):
        @pl.when(core == 0)
        def _():
            for d in range(1, 4):
                x_first(t, d).wait_recv()
            for j in range(2):
                middle[t, j] = (
                    (summed[t, 2 * x + j] + got_first[t, j])
                    + (got_first[t, 2 + j] + got_first[t, 4 + j])
                )
            y_second(t).start()

        @pl.when(core == 1)
        def _():
            y_first(t).wait_recv()
            for j in range(4):
                middle[t, j] = summed[t, 4 * y + j] + got_first[t, j]
            for d in (2, 1, 3):
                x_second(t, d).start()

    def third_stage(t):
        @pl.when(core == 0)
        def _():
            y_second(t).wait_recv()
            send_z[t] = middle[t, y] + got_second[t, 0]

        @pl.when(core == 1)
        def _():
            for d in range(1, 4):
                x_second(t, d).wait_recv()
            send_z[t] = (middle[t, x] + got_second[t, 0]) + (got_second[t, 1] + got_second[t, 2])

        z_copy(t).start()

    def plane_stage(t):
        core_copy(t).wait_recv()
        summed[t] = part[t, core] + got_core[t]
        for d in (6, 7, 5, 2, 3, 1, 4):
            plane_copy(t, d).start()

    def half_stage(half):
        half_copy(half).wait_recv()
        blocks = pl.ds(4 * half, 4)
        summed[last, blocks] = part[last, core, blocks] + got_core[last, blocks]

        @pl.when(y == half)
        def _():
            for d in (2, 3, 1):
                plane_copy(last, d).start()

        @pl.when(y != half)
        def _():
            for d in (6, 7, 5, 4):
                plane_copy(last, d).start()

    def plane_sum(t):
        for d in range(1, PLANE):
            plane_copy(t, d).wait_recv()
        block = summed[t, mine]
        for d in range(1, PLANE):
            block = block + got_plane[t - TWO_STEP, d - 1]
        return block

    def each(stage, first, end):
        def one(k, carry):
            stage(k)
            return carry

        lax.fori_loop(first, end, one, 0)

    last = Z - 1

    def rows_at(t, begin, count):
        start = pl.multiple_of(target(t) * CHUNK + begin, count)
        return rows_ref[:, pl.ds(start, count)]

    def step(t, carry):
        chunk = mixed_chunk(position, rows_at(t, 0, CHUNK), xs)
        for j in range(16):
            part[t, j % 2, j // 2] = chunk[:, j * BLOCK:(j + 1) * BLOCK]

        @pl.when(t == 0)
        def _():
            pl.semaphore_wait(barrier, len(known))

        core_copy(t).start()

        @pl.when((t >= 1) & (t < 4))
        def _():
            pl.semaphore_wait(greet.at[t - 1], 2)

        @pl.when(t < 3)
        def _():
            for to in beside:
                pl.semaphore_signal(greet.at[t], inc=1, device_id=to, device_id_type=MESH)

        @pl.when((t >= 1) & (t <= TWO_STEP))
        def _():
            first_stage(t - 1)

        @pl.when(t > TWO_STEP)
        def _():
            plane_stage(t - 1)

        @pl.when(t >= 3)
        def _():
            second_stage(t - 3)

        @pl.when(t >= 5)
        def _():
            third_stage(t - 5)

        return carry

    lax.fori_loop(0, last, step, 0)

    for half in range(2):
        chunk = mixed_chunk(position, rows_at(last, half * CHUNK // 2, CHUNK // 2), xs)
        for j in range(8):
            part[last, j % 2, 4 * half + j // 2] = chunk[:, j * BLOCK:(j + 1) * BLOCK]
        half_copy(half).start()
        if half == 0:
            plane_stage(last - 1)
            second_stage(4)
            third_stage(2)
        else:
            second_stage(5)
            half_stage(0)
            half_stage(1)

    each(third_stage, 3, TWO_STEP)
    for t in range(TWO_STEP, last):
        send_z[t] = plane_sum(t)
        z_copy(t).start()
    cross_copy().start()
    own = plane_sum(last)
    for t in range(last - 1):
        z_copy(t).wait_recv()
        own = own + got_z[t]
    early[...] = own

    def place(at):
        return pl.ds(pl.multiple_of(at * COLS, COLS), COLS)

    def col_copy():
        return copy(early, got_early, col_sem.at[0], col_sem.at[1], partner)

    col_copy().start()
    z_copy(last - 1).wait_recv()
    own = own + got_z[last - 1]
    sketch_ref[...] = own
    both[place(col), :] = own
    cross_copy().wait_recv()
    col_copy().wait_recv()
    both[place(1 - col), :] = got_early[...] + got_cross[...]
    gram_part[...] = lax.dot_general(
        own, both[...], (((1,), (1,)), ((), ())),
        precision=lax.Precision.HIGHEST, preferred_element_type=jnp.float32,
    ).reshape(PLANE, 8, 128)

    line = x * 2 + core

    def rs_copy(d):
        return copy(
            gram_part.at[line ^ d], got_rs.at[d - 1], rs_send.at[d - 1], rs_recv.at[d - 1], in_line(d)
        )

    for d in (4, 5, 2, 3, 6, 7, 1):
        rs_copy(d).start()
    for d in range(1, PLANE):
        rs_copy(d).wait_recv()
    piece = gram_part[line]
    for d in range(1, PLANE):
        piece = piece + got_rs[d - 1]
    me = z * 2 + y
    totals[me] = piece

    def tot_copy(k, at):
        return copy(totals.at[at], totals.at[at], tot_send.at[k - 1], tot_recv.at[k - 1], across(k))

    for k in (8, 7, 9, 6, 10, 5, 11, 4, 12, 3, 13, 2, 14, 1, 15):
        tot_copy(k, me).start()
    def drain(t, carry):
        core_copy(t).wait_send()
        return carry

    def drain_stages(t, carry):
        @pl.when(core == 0)
        def _():
            for d in range(1, 4):
                x_first(t, d).wait_send()
            y_second(t).wait_send()

        @pl.when(core == 1)
        def _():
            y_first(t).wait_send()
            for d in range(1, 4):
                x_second(t, d).wait_send()

        return carry

    lax.fori_loop(0, last, drain, 0)
    lax.fori_loop(0, TWO_STEP, drain_stages, 0)
    half_copy(0).wait_send()
    half_copy(1).wait_send()
    for t in range(last):
        z_copy(t).wait_send()
    cross_copy().wait_send()
    col_copy().wait_send()
    for d in range(1, PLANE):
        for t in range(TWO_STEP, Z):
            plane_copy(t, d).wait_send()
        rs_copy(d).wait_send()

    for k in range(1, 16):
        tot_copy(k, (me + 16 - k) % 16).wait_recv()
    piece = totals[0]
    for k in range(1, 16):
        piece = piece + totals[k]
    pieces[line] = piece * (1.0 / 16384.0)

    def out_copy(d, at):
        return copy(pieces.at[at], pieces.at[at], out_send.at[d - 1], out_recv.at[d - 1], in_line(d))

    for d in (4, 5, 2, 3, 6, 7, 1):
        out_copy(d, line).start()
    for k in range(1, 16):
        tot_copy(k, me).wait_send()
    for d in range(1, PLANE):
        out_copy(d, line ^ d).wait_recv()
    gram_ref[...] = pieces[...].reshape(COLS, 128)
    for d in range(1, PLANE):
        out_copy(d, line).wait_send()


def hand_over(sketch_ref, gram_ref, sketch_out, gram_out):
    sketch_out[...] = sketch_ref[...]
    gram_out[...] = gram_ref[...]


def body(matrix_panel, row_signs, sample_rows):
    vmem = pl.BlockSpec(memory_space=pltpu.VMEM)
    f32 = jnp.float32
    block = (COLS, BLOCK)
    sems = pltpu.SemaphoreType.DMA
    outs = (jax.ShapeDtypeStruct(block, f32), jax.ShapeDtypeStruct(block, f32))
    sketch, gram = pl.pallas_call(
        kernel,
        out_shape=outs,
        in_specs=[vmem] * 3,
        out_specs=(vmem, vmem),
        scratch_shapes=[
            pltpu.VMEM((SPLIT * COLS, DEPTH), jnp.bfloat16),
            pltpu.VMEM((Z, CORES, PLANE) + block, f32),
            pltpu.VMEM((Z, PLANE) + block, f32),
            pltpu.VMEM((Z, PLANE) + block, f32),
            pltpu.VMEM((TWO_STEP, 6) + block, f32),
            pltpu.VMEM((TWO_STEP, 4) + block, f32),
            pltpu.VMEM((TWO_STEP, 3) + block, f32),
            pltpu.VMEM((Z - TWO_STEP, PLANE - 1) + block, f32),
            pltpu.VMEM((Z - 1,) + block, f32),
            pltpu.VMEM((Z - 1,) + block, f32),
            pltpu.VMEM(block, f32),
            pltpu.VMEM(block, f32),
            pltpu.VMEM(block, f32),
            pltpu.VMEM((2 * COLS, BLOCK), f32),
            pltpu.VMEM((PLANE, 8, 128), f32),
            pltpu.VMEM((PLANE - 1, 8, 128), f32),
            pltpu.VMEM((16, 8, 128), f32),
            pltpu.VMEM((PLANE, 8, 128), f32),
            pltpu.SemaphoreType.REGULAR((3,)),
            sems((Z + 1,)), sems((Z + 1,)),
            sems((TWO_STEP, 3)), sems((TWO_STEP, 3)),
            sems((TWO_STEP, 3)), sems((TWO_STEP, 3)),
            sems((Z - TWO_STEP, PLANE - 1)), sems((Z - TWO_STEP, PLANE - 1)),
            sems((Z - 1,)), sems((Z - 1,)),
            sems((2,)), sems((2,)),
            sems((PLANE - 1,)), sems((PLANE - 1,)),
            sems((15,)), sems((15,)),
            sems((PLANE - 1,)), sems((PLANE - 1,)),
        ],
        compiler_params=pltpu.CompilerParams(
            collective_id=0, has_side_effects=True, vmem_limit_bytes=56 * 2**20
        ),
        cost_estimate=pl.CostEstimate(
            flops=2 * COLS * 8192 * 16384, bytes_accessed=2**21, transcendentals=0
        ),
    )(matrix_panel, row_signs.reshape(1, -1), sample_rows.reshape(1, -1))
    return pl.pallas_call(
        hand_over, out_shape=outs, in_specs=[vmem] * 2, out_specs=(vmem, vmem)
    )(sketch, gram)


def solution(mesh):
    return jax.shard_map(
        body,
        mesh=mesh,
        in_specs=(P("col", "row"), P("row"), P()),
        out_specs=(P("col", "row"), P("col", None)),
        check_vma=False,
    )
```

```python
import functools

import jax
import jax.numpy as jnp
from jax import lax
from jax.experimental import pallas as pl
from jax.experimental.pallas import tpu as pltpu
from jax.sharding import PartitionSpec as P

MESH = pl.DeviceIdType.MESH
Z = 8
PLANE = 8
CORES = 2
BLOCK = 128
COLS = 64
SPLIT = 4
DEPTH = 2048
CHUNK = PLANE * CORES * BLOCK
TWO_STEP = 6


def parity(value, shift):
    while shift:
        value = value ^ (value >> shift)
        shift //= 2
    return value & 1


def sign_of(odd):
    return (1 - 2 * odd).astype(jnp.float32)


def mixed_chunk(position, rows, x_ref):
    count = rows.shape[1]
    bit = lambda k: sign_of((rows >> k) & 1)
    wide = lambda k: jnp.broadcast_to(bit(k), (16, count)).astype(jnp.bfloat16)
    spread = jnp.broadcast_to(rows, (16, count))
    low = parity(spread & lax.broadcasted_iota(jnp.int32, (16, count), 0), 2)
    tiles = [sign_of(low).astype(jnp.bfloat16)]
    for k in range(4, 8):
        flip = wide(k)
        tiles = tiles + [tile * flip for tile in tiles]
    upper = [None]
    for k in range(8, 11):
        flip = wide(k)
        upper = upper + [flip if one is None else one * flip for one in upper]
    total = jnp.zeros((SPLIT * COLS, count), jnp.float32)
    for k, flip in enumerate(upper):
        signs = jnp.concatenate([tile if flip is None else tile * flip for tile in tiles], axis=0)
        total = total + jnp.dot(
            x_ref[:, k * 256:(k + 1) * 256], signs, preferred_element_type=jnp.float32
        )
    parts = [total[a * COLS:(a + 1) * COLS] for a in range(SPLIT)]
    for k in (11, 12):
        flip = bit(k)
        parts = [parts[2 * i] + flip * parts[2 * i + 1] for i in range(len(parts) // 2)]
    weight = sign_of(parity((rows >> 13) & position, 4)) * (1.0 / 1024.0)
    return parts[0] * weight


def kernel(
    x_ref, sign_ref, rows_ref, sketch_ref, gram_ref,
    xs, part, got_core, summed, got_first, middle, got_second, got_plane, send_z, got_z,
    got_cross, early, got_early, both, gram_part, got_rs, totals, pieces,
    greet, core_send, core_recv, first_send, first_recv, second_send, second_recv,
    plane_send, plane_recv, z_send, z_recv,
    cross_send, cross_recv, col_sem, rs_send, rs_recv, tot_send, tot_recv, out_send, out_recv,
):
    position = lax.axis_index("row")
    col = lax.axis_index("col")
    z = position // 16
    y = (position // 8) % 2
    x = (position // 2) % 4
    core = position % 2
    mine = y * 4 + x

    def device(z_at=z, y_at=y, x_at=x, core_at=core, col_at=col):
        return (((z_at * 2 + y_at) * 4 + x_at) * 2 + core_at, col_at)

    def in_plane(d):
        return device(y_at=y ^ (d // 4), x_at=x ^ (d % 4))

    def in_line(d):
        return device(x_at=x ^ (d // 2), core_at=core ^ (d % 2))

    def across(k):
        other = (z * 2 + y + k) % 16
        return device(z_at=other // 2, y_at=other % 2)

    partner = (position, 1 - col)

    barrier = pltpu.get_barrier_semaphore()
    beside = [device(z_at=(z + 1) % Z), device(z_at=(z + 7) % Z)]
    known = beside + [in_plane(d) for d in range(1, 8)]
    known += [in_line(d) for d in (1, 3, 5, 7)]
    known += [partner]
    for to in known:
        pl.semaphore_signal(barrier, inc=1, device_id=to, device_id_type=MESH)

    for a in range(SPLIT):
        window = slice(a * DEPTH, (a + 1) * DEPTH)
        signs = sign_ref[:, window].astype(jnp.float32).astype(jnp.bfloat16)
        xs[a * COLS:(a + 1) * COLS, :] = x_ref[:, window] * signs

    def copy(src, dst, send, recv, to):
        return pltpu.make_async_remote_copy(
            src_ref=src, dst_ref=dst, send_sem=send, recv_sem=recv,
            device_id=to, device_id_type=MESH,
        )

    def target(t):
        return (z + jnp.where(t % 2 == 0, 4 + t // 2, 4 - (t + 1) // 2)) % Z

    def core_copy(t):
        return copy(
            part.at[t, 1 - core], got_core.at[t], core_send.at[t], core_recv.at[t],
            device(core_at=1 - core),
        )

    def half_copy(half):
        blocks = pl.ds(4 * half, 4)
        return copy(
            part.at[Z - 1, 1 - core, blocks], got_core.at[Z - 1, blocks],
            core_send.at[Z - 1 + half], core_recv.at[Z - 1 + half], device(core_at=1 - core),
        )

    def x_first(t, d):
        return copy(
            summed.at[t, pl.ds(2 * (x ^ d), 2)], got_first.at[t, pl.ds(2 * (d - 1), 2)],
            first_send.at[t, d - 1], first_recv.at[t, d - 1], device(x_at=x ^ d),
        )

    def y_second(t):
        return copy(
            middle.at[t, 1 - y], got_second.at[t, 0],
            second_send.at[t, 0], second_recv.at[t, 0], device(y_at=1 - y),
        )

    def y_first(t):
        return copy(
            summed.at[t, pl.ds(4 * (1 - y), 4)], got_first.at[t, pl.ds(0, 4)],
            first_send.at[t, 0], first_recv.at[t, 0], device(y_at=1 - y),
        )

    def x_second(t, d):
        return copy(
            middle.at[t, x ^ d], got_second.at[t, d - 1],
            second_send.at[t, d - 1], second_recv.at[t, d - 1], device(x_at=x ^ d),
        )

    def plane_copy(t, d):
        return copy(
            summed.at[t, mine ^ d], got_plane.at[t - TWO_STEP, d - 1],
            plane_send.at[t - TWO_STEP, d - 1], plane_recv.at[t - TWO_STEP, d - 1], in_plane(d),
        )

    def cross_copy(t):
        at = t - (Z - 3)
        return copy(
            send_z.at[t], got_cross.at[at], cross_send.at[at], cross_recv.at[at],
            device(z_at=target(t), col_at=1 - col),
        )

    def z_copy(t):
        return copy(
            send_z.at[t], got_z.at[t], z_send.at[t], z_recv.at[t], device(z_at=target(t))
        )

    def first_stage(t):
        core_copy(t).wait_recv()

        @pl.when(core == 0)
        def _():
            for j in range(PLANE):
                summed[t, (j % 4) * 2 + j // 4] = part[t, 0, j] + got_core[t, j]
            for d in (2, 1, 3):
                x_first(t, d).start()

        @pl.when(core == 1)
        def _():
            for j in range(PLANE):
                summed[t, j] = part[t, 1, j] + got_core[t, j]
            y_first(t).start()

    def second_stage(t):
        @pl.when(core == 0)
        def _():
            for d in range(1, 4):
                x_first(t, d).wait_recv()
            for j in range(2):
                middle[t, j] = (
                    (summed[t, 2 * x + j] + got_first[t, j])
                    + (got_first[t, 2 + j] + got_first[t, 4 + j])
                )
            y_second(t).start()

        @pl.when(core == 1)
        def _():
            y_first(t).wait_recv()
            for j in range(4):
                middle[t, j] = summed[t, 4 * y + j] + got_first[t, j]
            for d in (2, 1, 3):
                x_second(t, d).start()

    def third_stage(t):
        @pl.when(core == 0)
        def _():
            y_second(t).wait_recv()
            send_z[t] = middle[t, y] + got_second[t, 0]

        @pl.when(core == 1)
        def _():
            for d in range(1, 4):
                x_second(t, d).wait_recv()
            send_z[t] = (middle[t, x] + got_second[t, 0]) + (got_second[t, 1] + got_second[t, 2])

        z_copy(t).start()

    def plane_stage(t):
        core_copy(t).wait_recv()
        summed[t] = part[t, core] + got_core[t]
        for d in (6, 7, 5, 2, 3, 1, 4):
            plane_copy(t, d).start()

    def half_stage(half):
        half_copy(half).wait_recv()
        blocks = pl.ds(4 * half, 4)
        summed[last, blocks] = part[last, core, blocks] + got_core[last, blocks]

        @pl.when(y == half)
        def _():
            for d in (2, 3, 1):
                plane_copy(last, d).start()

        @pl.when(y != half)
        def _():
            for d in (6, 7, 5, 4):
                plane_copy(last, d).start()

    def plane_sum(t):
        for d in range(1, PLANE):
            plane_copy(t, d).wait_recv()
        block = summed[t, mine]
        for d in range(1, PLANE):
            block = block + got_plane[t - TWO_STEP, d - 1]
        return block

    def each(stage, first, end):
        def one(k, carry):
            stage(k)
            return carry

        lax.fori_loop(first, end, one, 0)

    last = Z - 1

    def rows_at(t, begin, count):
        start = pl.multiple_of(target(t) * CHUNK + begin, count)
        return rows_ref[:, pl.ds(start, count)]

    def step(t, carry):
        chunk = mixed_chunk(position, rows_at(t, 0, CHUNK), xs)
        for j in range(16):
            part[t, j % 2, j // 2] = chunk[:, j * BLOCK:(j + 1) * BLOCK]

        @pl.when(t == 0)
        def _():
            pl.semaphore_wait(barrier, len(known))

        core_copy(t).start()

        @pl.when((t >= 1) & (t < 4))
        def _():
            pl.semaphore_wait(greet.at[t - 1], 2)

        @pl.when(t < 3)
        def _():
            for to in beside:
                pl.semaphore_signal(greet.at[t], inc=1, device_id=to, device_id_type=MESH)

        @pl.when((t >= 1) & (t <= TWO_STEP))
        def _():
            first_stage(t - 1)

        @pl.when(t > TWO_STEP)
        def _():
            plane_stage(t - 1)

        @pl.when(t >= 3)
        def _():
            second_stage(t - 3)

        @pl.when(t >= 5)
        def _():
            third_stage(t - 5)

        return carry

    lax.fori_loop(0, last, step, 0)

    for half in range(2):
        chunk = mixed_chunk(position, rows_at(last, half * CHUNK // 2, CHUNK // 2), xs)
        for j in range(8):
            part[last, j % 2, 4 * half + j // 2] = chunk[:, j * BLOCK:(j + 1) * BLOCK]
        half_copy(half).start()
        if half == 0:
            plane_stage(last - 1)
            second_stage(4)
            third_stage(2)
        else:
            second_stage(5)
            half_stage(0)
            half_stage(1)

    each(third_stage, 3, TWO_STEP)
    cross_copy(last - 2).start()
    for t in range(TWO_STEP, last):
        send_z[t] = plane_sum(t)
        z_copy(t).start()
    cross_copy(last - 1).start()
    own = plane_sum(last)
    for t in range(last - 2):
        z_copy(t).wait_recv()
        own = own + got_z[t]
    early[...] = own

    def place(at):
        return pl.ds(pl.multiple_of(at * COLS, COLS), COLS)

    def col_copy():
        return copy(early, got_early, col_sem.at[0], col_sem.at[1], partner)

    col_copy().start()
    for t in range(last - 2, last):
        z_copy(t).wait_recv()
        own = own + got_z[t]
    sketch_ref[...] = own
    both[place(col), :] = own
    cross_copy(last - 2).wait_recv()
    cross_copy(last - 1).wait_recv()
    col_copy().wait_recv()
    both[place(1 - col), :] = (got_early[...] + got_cross[0]) + got_cross[1]
    gram_part[...] = lax.dot_general(
        own, both[...], (((1,), (1,)), ((), ())),
        precision=lax.Precision.HIGHEST, preferred_element_type=jnp.float32,
    ).reshape(PLANE, 8, 128)

    line = x * 2 + core

    def rs_copy(d):
        return copy(
            gram_part.at[line ^ d], got_rs.at[d - 1], rs_send.at[d - 1], rs_recv.at[d - 1], in_line(d)
        )

    for d in (4, 5, 2, 3, 6, 7, 1):
        rs_copy(d).start()
    for d in range(1, PLANE):
        rs_copy(d).wait_recv()
    piece = gram_part[line]
    for d in range(1, PLANE):
        piece = piece + got_rs[d - 1]
    me = z * 2 + y
    totals[me] = piece

    def tot_copy(k, at):
        return copy(totals.at[at], totals.at[at], tot_send.at[k - 1], tot_recv.at[k - 1], across(k))

    for k in (8, 7, 9, 6, 10, 5, 11, 4, 12, 3, 13, 2, 14, 1, 15):
        tot_copy(k, me).start()
    def drain(t, carry):
        core_copy(t).wait_send()
        return carry

    def drain_stages(t, carry):
        @pl.when(core == 0)
        def _():
            for d in range(1, 4):
                x_first(t, d).wait_send()
            y_second(t).wait_send()

        @pl.when(core == 1)
        def _():
            y_first(t).wait_send()
            for d in range(1, 4):
                x_second(t, d).wait_send()

        return carry

    lax.fori_loop(0, last, drain, 0)
    lax.fori_loop(0, TWO_STEP, drain_stages, 0)
    half_copy(0).wait_send()
    half_copy(1).wait_send()
    for t in range(last):
        z_copy(t).wait_send()
    cross_copy(last - 2).wait_send()
    cross_copy(last - 1).wait_send()
    col_copy().wait_send()
    for d in range(1, PLANE):
        for t in range(TWO_STEP, Z):
            plane_copy(t, d).wait_send()
        rs_copy(d).wait_send()

    for k in range(1, 16):
        tot_copy(k, (me + 16 - k) % 16).wait_recv()
    piece = totals[0]
    for k in range(1, 16):
        piece = piece + totals[k]
    pieces[line] = piece * (1.0 / 16384.0)

    def out_copy(d, at):
        return copy(pieces.at[at], pieces.at[at], out_send.at[d - 1], out_recv.at[d - 1], in_line(d))

    for d in (4, 5, 2, 3, 6, 7, 1):
        out_copy(d, line).start()
    for k in range(1, 16):
        tot_copy(k, me).wait_send()
    for d in range(1, PLANE):
        out_copy(d, line ^ d).wait_recv()
    gram_ref[...] = pieces[...].reshape(COLS, 128)
    for d in range(1, PLANE):
        out_copy(d, line).wait_send()


def hand_over(sketch_ref, gram_ref, sketch_out, gram_out):
    sketch_out[...] = sketch_ref[...]
    gram_out[...] = gram_ref[...]


def body(matrix_panel, row_signs, sample_rows):
    vmem = pl.BlockSpec(memory_space=pltpu.VMEM)
    f32 = jnp.float32
    block = (COLS, BLOCK)
    sems = pltpu.SemaphoreType.DMA
    outs = (jax.ShapeDtypeStruct(block, f32), jax.ShapeDtypeStruct(block, f32))
    sketch, gram = pl.pallas_call(
        kernel,
        out_shape=outs,
        in_specs=[vmem] * 3,
        out_specs=(vmem, vmem),
        scratch_shapes=[
            pltpu.VMEM((SPLIT * COLS, DEPTH), jnp.bfloat16),
            pltpu.VMEM((Z, CORES, PLANE) + block, f32),
            pltpu.VMEM((Z, PLANE) + block, f32),
            pltpu.VMEM((Z, PLANE) + block, f32),
            pltpu.VMEM((TWO_STEP, 6) + block, f32),
            pltpu.VMEM((TWO_STEP, 4) + block, f32),
            pltpu.VMEM((TWO_STEP, 3) + block, f32),
            pltpu.VMEM((Z - TWO_STEP, PLANE - 1) + block, f32),
            pltpu.VMEM((Z - 1,) + block, f32),
            pltpu.VMEM((Z - 1,) + block, f32),
            pltpu.VMEM((2,) + block, f32),
            pltpu.VMEM(block, f32),
            pltpu.VMEM(block, f32),
            pltpu.VMEM((2 * COLS, BLOCK), f32),
            pltpu.VMEM((PLANE, 8, 128), f32),
            pltpu.VMEM((PLANE - 1, 8, 128), f32),
            pltpu.VMEM((16, 8, 128), f32),
            pltpu.VMEM((PLANE, 8, 128), f32),
            pltpu.SemaphoreType.REGULAR((3,)),
            sems((Z + 1,)), sems((Z + 1,)),
            sems((TWO_STEP, 3)), sems((TWO_STEP, 3)),
            sems((TWO_STEP, 3)), sems((TWO_STEP, 3)),
            sems((Z - TWO_STEP, PLANE - 1)), sems((Z - TWO_STEP, PLANE - 1)),
            sems((Z - 1,)), sems((Z - 1,)),
            sems((2,)), sems((2,)), sems((2,)),
            sems((PLANE - 1,)), sems((PLANE - 1,)),
            sems((15,)), sems((15,)),
            sems((PLANE - 1,)), sems((PLANE - 1,)),
        ],
        compiler_params=pltpu.CompilerParams(
            collective_id=0, has_side_effects=True, vmem_limit_bytes=56 * 2**20
        ),
        cost_estimate=pl.CostEstimate(
            flops=2 * COLS * 8192 * 16384, bytes_accessed=2**21, transcendentals=0
        ),
    )(matrix_panel, row_signs.reshape(1, -1), sample_rows.reshape(1, -1))
    return pl.pallas_call(
        hand_over, out_shape=outs, in_specs=[vmem] * 2, out_specs=(vmem, vmem)
    )(sketch, gram)


def solution(mesh):
    return jax.shard_map(
        body,
        mesh=mesh,
        in_specs=(P("col", "row"), P("row"), P()),
        out_specs=(P("col", "row"), P("col", None)),
        check_vma=False,
    )
```
